32 devices in a mesh: areal: 8 (over y, x, core), layer: 4 (over z).
Axes of the slice: x: 2, y: 2, z: 4, core: 2. Of those that a mesh axis runs over, the one named last changes fastest.
Arguments:
- pressure: float32 [32, 2048, 256], P('layer', 'areal'), may hold values from -6 to 6
- saturations: float32 [2, 32, 2048, 256], P(None, 'layer', 'areal'), may hold values from 0.05 to 0.4
- old_saturations: float32 [2, 32, 2048, 256], P(None, 'layer', 'areal'), may hold values from 0.05 to 0.4
- permeability: float32 [32, 2048, 256], P('layer', 'areal'), may hold values from 0.05 to 5
- pore_volume: float32 [32, 2048, 256], P('layer', 'areal'), may hold values from 0.5 to 2
- perf_cell: int32 [4, 8, 8, 256], P('layer', 'areal'), may hold values from 0 to 65535
- perf_layer: int32 [4, 8, 8, 256], P('layer', 'areal'), may hold values from 0 to 7
- perf_seg: int32 [4, 8, 8, 256], P('layer', 'areal'), may hold values from 0 to 383
- perf_index: float32 [4, 8, 8, 256], P('layer', 'areal'), may hold values from 0.5 to 4
- perf_blocks: int32 [4, 8, 8], P('layer', 'areal'), may hold values from 0 to 2, as said below
- seg_parent: int32 [1536, 8], P('areal'), may hold values from 0 to 6, as said below
- seg_cond: float32 [1536, 8], P('areal'), may hold values from 10 to 100
- seg_target: float32 [1536, 8], P('areal'), may hold values from -6 to 6
Outputs:
- cell_residual: float32 [3, 32, 2048, 256], P(None, 'layer', 'areal')
- well_pressure: float32 [1536, 8], P('areal', 'layer')
The draws below stay inside these ranges and needn't reach their ends.
Inputs may be any that keep to these rules, and one draw needn't show every extreme that they name: `perf_blocks`: in every layer one owner index, drawn from the seed, has 2 live blocks from every areal index. Apart from it, each owner has 2 live blocks from its own areal index, 1 to 2 from the areal indices next to it (circularly), and 0 to 1 from the others. `seg_parent`: segment 0 has parent 0; every other segment's parent is a lower segment of the same well.
All inputs are finite; a program needn't handle non-finite values.
Results may differ from the reference program's by a relative error of at most 0.0003.
Values sent between devices are 32-bit elements; how exact they have to be, the bound alone decides.
A program may use at most 192 MiB of HBM per device.

```python
import math
import jax
import jax.numpy as jnp
from jax import lax

CZ = 8
CX = 256
CY = 256
WELLS_DEV = 192
SEG_SLAB = 2
BLOCK = 128
CAP_BLK = 2
NZ = 32
NX = 2048
NY = 256
SEG = 8
WELLS = 1536
SLOTS = 256
COLUMNS = 65536
WELL_SEGS = 384
N_AREAL = 8
N_LAYER = 4


def draw_perf_blocks(key, part):
    layers = SEG // SEG_SLAB
    owners = WELLS // WELLS_DEV
    first_key, second_key, third_key = jax.random.split(jax.random.fold_in(key, 11), 3)
    far_counts = jax.random.randint(first_key, (layers, owners, owners), 0, CAP_BLK // 2 + 1)
    near_counts = jax.random.randint(third_key, (layers, owners, owners), CAP_BLK // 2, CAP_BLK + 1)
    hot_owner = jax.random.randint(second_key, (layers,), 0, owners)
    owner_ids = jnp.arange(owners, dtype=jnp.int32)
    gap = (owner_ids[None, :] - owner_ids[:, None]) % owners
    distance = jnp.minimum(gap, owners - gap)
    counts = jnp.where(distance[None] == 0, CAP_BLK, jnp.where(distance[None] == 1, near_counts, far_counts))
    return jnp.where(owner_ids[None, None, :] == hot_owner[:, None, None], CAP_BLK, counts).astype(jnp.int32)


def draw_seg_parent(key, part):
    raw_bits = jax.random.randint(jax.random.fold_in(key, 23), (WELLS, SEG), 0, 2 ** 30)
    positions = jnp.arange(SEG, dtype=jnp.int32)[None, :]
    return jnp.where(positions > 0, raw_bits % jnp.maximum(positions, 1), 0).astype(jnp.int32)


def set_ends(entries, stream_key, low, high):
    extent = entries.shape
    index_at = [jax.random.randint(jax.random.fold_in(stream_key, axis), (), 0, extent[axis]) for axis in range(len(extent))]
    entries = entries.at[tuple(index_at)].set(low)
    longest = extent.index(max(extent))
    index_at[longest] = (index_at[longest] + 1) % extent[longest]
    return entries.at[tuple(index_at)].set(high)


def steps_of(key, extent, shards, smallest, largest):
    gain, own = 1.0, jax.random.fold_in(key, 6)
    for axis_at, parts in shards:
        heights = jnp.exp(jax.random.uniform(jax.random.fold_in(own, axis_at), (parts,), jnp.float32, smallest / len(shards), largest / len(shards)))
        gain = gain * jnp.repeat(heights, extent[axis_at] // parts).reshape([-1 if axis == axis_at else 1 for axis in range(len(extent))])
    return gain


def centred(rng, extent, scale, bound, pieces=(), kind=jnp.bfloat16):
    loudness = steps_of(rng, extent, pieces, -0.22, 0.18) if pieces else 1.0
    drawn = jax.random.normal(rng, extent, jnp.float32) * scale * loudness
    return jnp.minimum(jnp.maximum(drawn, -bound), bound).astype(kind)


def setup_inputs(seed: int = 0) -> dict:
    key_of = jax.random.split(jax.random.key(seed), 14)
    return {
        "pressure": centred(key_of[0], (NZ, NX, NY), 1.0, 6.0, ((0, 4), (1, 8)), jnp.float32),
        "saturations": jnp.clip(0.05 + 0.35 * jax.random.uniform(key_of[1], (2, NZ, NX, NY), jnp.float32) ** steps_of(key_of[1], (2, NZ, NX, NY), ((1, 4), (2, 8)), -0.2, 0.2), 0.05, 0.4),
        "old_saturations": jnp.clip(0.05 + 0.35 * jax.random.uniform(key_of[2], (2, NZ, NX, NY), jnp.float32) ** steps_of(key_of[2], (2, NZ, NX, NY), ((1, 4), (2, 8)), -0.2, 0.2), 0.05, 0.4),
        "permeability": jnp.clip(jnp.exp(math.log(5.0) - 4.6051702 * jax.random.uniform(key_of[3], (NZ, NX, NY), jnp.float32) ** steps_of(key_of[3], (NZ, NX, NY), ((0, 4), (1, 8)), -0.2, 0.2)), 0.05, 5.0),
        "pore_volume": jnp.clip(jnp.exp(math.log(2.0) - 1.3862944 * jax.random.uniform(key_of[4], (NZ, NX, NY), jnp.float32) ** steps_of(key_of[4], (NZ, NX, NY), ((0, 4), (1, 8)), -0.2, 0.2)), 0.5, 2.0),
        "perf_cell": set_ends(jax.random.randint(key_of[5], (N_LAYER, N_AREAL, N_AREAL, SLOTS), 0, COLUMNS), jax.random.fold_in(key_of[5], 1), 0, COLUMNS - 1).astype(jnp.int32),
        "perf_layer": set_ends(jax.random.randint(key_of[6], (N_LAYER, N_AREAL, N_AREAL, SLOTS), 0, CZ), jax.random.fold_in(key_of[6], 1), 0, CZ - 1).astype(jnp.int32),
        "perf_seg": set_ends(jax.random.randint(key_of[7], (N_LAYER, N_AREAL, N_AREAL, SLOTS), 0, WELL_SEGS), jax.random.fold_in(key_of[7], 1), 0, WELL_SEGS - 1).astype(jnp.int32),
        "perf_index": jnp.clip(jnp.exp(math.log(4.0) - 2.0794415 * jax.random.uniform(key_of[8], (N_LAYER, N_AREAL, N_AREAL, SLOTS), jnp.float32) ** steps_of(key_of[8], (N_LAYER, N_AREAL, N_AREAL, SLOTS), ((0, 4), (1, 8)), -0.2, 0.2)), 0.5, 4.0),
        "perf_blocks": draw_perf_blocks(jax.random.fold_in(key_of[13], 71), 0),
        "seg_parent": draw_seg_parent(jax.random.fold_in(key_of[13], 71), 0),
        "seg_cond": jnp.clip(jnp.exp(math.log(100.0) - 2.3025851 * jax.random.uniform(key_of[11], (WELLS, SEG), jnp.float32) ** steps_of(key_of[11], (WELLS, SEG), ((0, 8),), -0.2, 0.2)), 10.0, 100.0),
        "seg_target": centred(key_of[12], (WELLS, SEG), 1.0, 6.0, ((0, 8),), jnp.float32),
    }


MU_WATER = 0.5
MU_OIL = 2.0
MU_GAS = 0.2
GRAVITY = (0.35, 0.28, 0.07)
GEOMETRY = (0.4, 1.0, 1.0)
RELAX = 20.0

def mobilities(water, gas_sat):
    oil_sat = 1.0 - water - gas_sat
    return jnp.stack([water * water / MU_WATER, oil_sat * oil_sat / MU_OIL, gas_sat * gas_sat / MU_GAS])

def face(values, direction, offset, face_count):
    picks = [slice(1, -1), slice(1, -1), slice(1, -1)]
    picks[direction] = slice(offset, offset + face_count)
    leading = (slice(None),) * (values.ndim - 3)
    return values[leading + tuple(picks)]

def divergence(padded, lam_pad):
    press = padded[0]
    perm = padded[3]
    gravity = jnp.array(GRAVITY, dtype=press.dtype)[:, None, None, None]
    result = None
    for direction in range(3):
        face_count = press.shape[direction] - 1
        perm_left = face(perm, direction, 0, face_count)
        perm_right = face(perm, direction, 1, face_count)
        transmiss = GEOMETRY[direction] * 2.0 * perm_left * perm_right / (perm_left + perm_right)
        pressure_drop = face(press, direction, 0, face_count) - face(press, direction, 1, face_count)
        potential = pressure_drop[None] + (gravity if direction == 0 else 0.0 * gravity)
        mob_left = face(lam_pad, direction, 0, face_count)
        mob_right = face(lam_pad, direction, 1, face_count)
        upwind = jnp.where(potential > 0, mob_left, mob_right)
        face_flux = transmiss[None] * upwind * potential
        outflow = lax.slice_in_dim(face_flux, 1, face_count, axis=direction + 1) - lax.slice_in_dim(face_flux, 0, face_count - 1, axis=direction + 1)
        result = outflow if result is None else result + outflow
    return result

def solve_wells(seg_mobility, seg_weighted, seg_parent, seg_cond, seg_target):
    nseg = seg_parent.shape[1]
    positions = jnp.arange(nseg, dtype=jnp.int32)
    incidence = (positions[None, :, None] == positions[None, None, :]).astype(seg_cond.dtype) - (seg_parent[:, :, None] == positions[None, None, :]).astype(seg_cond.dtype)
    weight = seg_cond * (positions > 0).astype(seg_cond.dtype)[None, :]
    laplacian = jnp.einsum('bsi,bs,bsj->bij', incidence, weight, incidence, precision=lax.Precision.HIGHEST)
    matrix = laplacian + (seg_mobility + RELAX)[:, :, None] * jnp.eye(nseg, dtype=seg_cond.dtype)[None]
    right_side = seg_weighted + RELAX * seg_target
    factor = jnp.linalg.cholesky(matrix)
    return jax.scipy.linalg.cho_solve((factor, True), right_side[:, :, None])[:, :, 0]

def to_blocks(values):
    return values.reshape(N_LAYER, CZ, N_AREAL, CX, CY).transpose(0, 2, 1, 3, 4).reshape(N_LAYER, N_AREAL, CZ * CX * CY)

def from_blocks(values):
    return values.reshape(N_LAYER, N_AREAL, CZ, CX, CY).transpose(0, 2, 1, 3, 4).reshape(NZ, NX, NY)

def reference(pressure, saturations, old_saturations, permeability, pore_volume, perf_cell, perf_layer, perf_seg, perf_index, perf_blocks, seg_parent, seg_cond, seg_target):
    fields = jnp.concatenate([pressure[None], saturations, permeability[None]], axis=0)
    padded = jnp.pad(fields, ((0, 0), (1, 1), (1, 1), (1, 1)))
    lam_pad = mobilities(padded[1], padded[2])
    net_flow = divergence(padded, lam_pad)
    mobility = lam_pad[:, 1:-1, 1:-1, 1:-1]
    press_blocks = to_blocks(pressure)
    mob_blocks = jnp.stack([to_blocks(mobility[phase]) for phase in range(3)])
    slot_count = perf_cell.shape[3]
    block_cell = (perf_layer * (CX * CY) + perf_cell).astype(jnp.int32)
    flat_cells = block_cell.reshape(N_LAYER, N_AREAL, N_AREAL * slot_count)
    perf_press = jnp.take_along_axis(press_blocks, flat_cells, axis=2).reshape(perf_cell.shape)
    perf_mob = jnp.take_along_axis(mob_blocks, flat_cells[None], axis=3).reshape((3,) + perf_cell.shape)
    live_mask = (jnp.arange(slot_count, dtype=jnp.int32)[None, None, None, :] < perf_blocks[..., None] * BLOCK).astype(pressure.dtype)
    weighted = (perf_index * live_mask)[None] * perf_mob
    mobile_sum = weighted[0] + weighted[1] + weighted[2]
    owner_ids = jnp.arange(N_AREAL, dtype=jnp.int32)[None, None, :, None]
    layer_ids = jnp.arange(N_LAYER, dtype=jnp.int32)[:, None, None, None]
    source_ids = jnp.arange(N_AREAL, dtype=jnp.int32)[None, :, None, None]
    global_seg = ((owner_ids * WELLS_DEV + perf_seg // SEG_SLAB) * SEG + layer_ids * SEG_SLAB + perf_seg % SEG_SLAB).reshape(-1).astype(jnp.int32)
    seg_mobility = jax.ops.segment_sum(mobile_sum.reshape(-1), global_seg, WELLS * SEG).reshape(WELLS, SEG)
    seg_weighted = jax.ops.segment_sum((mobile_sum * perf_press).reshape(-1), global_seg, WELLS * SEG).reshape(WELLS, SEG)
    well_pressure = solve_wells(seg_mobility, seg_weighted, seg_parent, seg_cond, seg_target)
    perf_well = well_pressure.reshape(-1)[global_seg].reshape(perf_cell.shape)
    perf_rates = weighted * (perf_press - perf_well)[None]
    cell_ids = ((layer_ids * N_AREAL + source_ids) * (CZ * CX * CY) + block_cell).reshape(-1).astype(jnp.int32)
    inflow = jnp.stack([from_blocks(jax.ops.segment_sum(perf_rates[phase].reshape(-1), cell_ids, N_LAYER * N_AREAL * CZ * CX * CY)) for phase in range(3)])
    water = saturations[0]
    gas_sat = saturations[1]
    states = jnp.stack([water, 1.0 - water - gas_sat, gas_sat])
    old_states = jnp.stack([old_saturations[0], 1.0 - old_saturations[0] - old_saturations[1], old_saturations[1]])
    cell_residual = pore_volume[None] * (states - old_states) + net_flow + inflow
    return (cell_residual, well_pressure)
```

```python
import functools

import jax
import jax.numpy as jnp
from jax import lax
from jax.experimental import pallas as pl
from jax.experimental.pallas import tpu as pltpu
from jax.sharding import PartitionSpec as P

BLOCK = 128
LANES = 128

MU_WATER = 0.5
MU_OIL = 2.0
MU_GAS = 0.2
GRAVITY = (0.35, 0.28, 0.07)
GEOMETRY = (0.4, 1.0, 1.0)
RELAX = 20.0

VMEM = pltpu.VMEM
SMEM = pltpu.SMEM
MESH = pl.DeviceIdType.MESH
VLIMIT = 56 * 1024 * 1024


def mobilities(water, gas_sat):
    oil_sat = 1.0 - water - gas_sat
    return (
        water * water * (1.0 / MU_WATER),
        oil_sat * oil_sat * (1.0 / MU_OIL),
        gas_sat * gas_sat * (1.0 / MU_GAS),
    )


def pieces(value):
    high = value.astype(jnp.bfloat16).astype(jnp.float32)
    rest = value - high
    mid = rest.astype(jnp.bfloat16).astype(jnp.float32)
    return high, mid, rest - mid


def panel_index(seg, slab, width):
    return (seg % slab) * width + seg // slab


def tall(value, rows):
    return jnp.concatenate(
        [value, jnp.zeros((rows - value.shape[0], value.shape[1]), value.dtype)], axis=0
    )


def column_part(row, part, halves):
    value = row[:, :LANES]
    for h in range(1, halves):
        value = jnp.where(part == h, row[:, h * LANES : (h + 1) * LANES], value)
    return value


def gather_kernel(
    slab, width, halves, flat_s, blocks_s, press, sats, flat, seg, index, blocks,
    sums, perf_press, perf_weight, rows,
):
    groups, slots = flat.shape
    for owner in range(groups):
        for block in range(slots // BLOCK):
            base = owner * slots + block * BLOCK

            @pl.when(blocks_s[owner] > block)
            def _(base=base, owner=owner, block=block):
                def step(i, carry):
                    for j in range(16):
                        at = i * 16 + j
                        number = flat_s[owner, block * BLOCK + at] // LANES
                        row = pl.ds(number // halves, 1)
                        part = number % halves
                        here = pl.ds(base + at, 1)
                        rows[0, here, :] = column_part(press[row, :], part, halves)
                        rows[1, here, :] = column_part(sats[0, row, :], part, halves)
                        rows[2, here, :] = column_part(sats[1, row, :], part, halves)
                    return carry

                lax.fori_loop(0, BLOCK // 16, step, 0)

    lanes_t = jnp.transpose(tall(flat[...] % LANES, LANES))
    lane = lax.broadcasted_iota(jnp.int32, (slots, LANES), 1)
    picked = jnp.zeros((slots, LANES), jnp.float32)
    for owner in range(groups):
        mask = lane == lanes_t[:, owner : owner + 1]
        for field in range(3):
            row = rows[field, owner * slots : (owner + 1) * slots, :]
            value = jnp.sum(jnp.where(mask, row, 0.0), axis=1, keepdims=True)
            picked = jnp.where(lane == field * groups + owner, value, picked)
    picked = jnp.transpose(picked)
    live = lax.broadcasted_iota(jnp.int32, (groups, slots), 1) < blocks[...] * BLOCK
    pressure = jnp.where(live, picked[0:groups], 0.0)
    water = picked[groups : 2 * groups]
    gas_sat = picked[2 * groups : 3 * groups]
    weight = jnp.where(live, index[...], 0.0)
    lam = mobilities(water, gas_sat)
    mobile = jnp.where(live, weight * lam[0] + weight * lam[1] + weight * lam[2], 0.0)
    perf_press[...] = pressure
    perf_weight[...] = weight
    parts = pieces(mobile) + pieces(mobile * pressure)
    target = panel_index(seg[...], slab, width)
    bins = lax.broadcasted_iota(jnp.int32, (slab * width, slots), 0)
    zero = jnp.zeros((2, slots), jnp.float32)
    chunks = slab * width // LANES
    for owner in range(groups):
        left = jnp.concatenate([part[owner : owner + 1] for part in parts] + [zero], axis=0)
        hot = jnp.where(bins == target[owner : owner + 1], 1.0, 0.0).astype(jnp.bfloat16)
        total = lax.dot_general(
            left.astype(jnp.bfloat16), hot, (((1,), (1,)), ((), ())),
            preferred_element_type=jnp.float32,
        )
        for kind in range(2):
            line = total[3 * kind : 3 * kind + 1] + total[3 * kind + 1 : 3 * kind + 2]
            line = line + total[3 * kind + 2 : 3 * kind + 3]
            for c in range(chunks):
                sums[owner, kind * chunks + c : kind * chunks + c + 1, :] = line[
                    :, c * LANES : (c + 1) * LANES
                ]


def wells_kernel(
    groups, layers, slab, width, sums, params, first, last,
    table, own_slab, before, after,
    got, panel, solved, send_a, recv_a, send_l, recv_l, send_p, recv_p, send_x, recv_x,
):
    area = lax.axis_index("areal")
    layer = lax.axis_index("layer")
    nseg = layers * slab
    half = width // LANES

    def areal_peer(d):
        return {"areal": lax.rem(area + d, groups)}

    def layer_peer(d):
        return {"layer": lax.rem(layer + d, layers)}

    barrier = pltpu.get_barrier_semaphore()
    for d in range(1, groups):
        pl.semaphore_signal(barrier, inc=1, device_id=areal_peer(d), device_id_type=MESH)
    for d in range(1, layers):
        pl.semaphore_signal(barrier, inc=1, device_id=layer_peer(d), device_id_type=MESH)
    pl.semaphore_wait(barrier, groups + layers - 2)

    to_owner = []
    for d in range(1, groups):
        copy = pltpu.make_async_remote_copy(
            sums.at[lax.rem(area + d, groups)], got.at[d], send_a.at[d], recv_a.at[d],
            device_id=areal_peer(d), device_id_type=MESH,
        )
        copy.start()
        to_owner.append(copy)
    halo = [
        pltpu.make_async_remote_copy(
            last, before, send_x.at[0], recv_x.at[0],
            device_id=areal_peer(1), device_id_type=MESH,
        ),
        pltpu.make_async_remote_copy(
            first, after, send_x.at[1], recv_x.at[1],
            device_id=areal_peer(groups - 1), device_id_type=MESH,
        ),
    ]
    for copy in halo:
        copy.start()

    total = sums[area]
    for d in range(1, groups):
        to_owner[d - 1].wait_recv()
        total = total + got[d]
    panel[layer] = total
    to_layers = []
    for d in range(1, layers):
        copy = pltpu.make_async_remote_copy(
            panel.at[layer], panel.at[layer], send_l.at[d], recv_l.at[d],
            device_id=layer_peer(d), device_id_type=MESH,
        )
        copy.start()
        to_layers.append(copy)
    for copy in to_layers:
        copy.wait_recv()

    def lines(kind):
        out = []
        for j in range(layers):
            tile = panel[j]
            for s in range(slab):
                at = (kind * slab + s) * half
                out.append(
                    jnp.concatenate([tile[at + h : at + h + 1] for h in range(half)], axis=1)
                )
        return jnp.concatenate(out, axis=0)

    excess = lines(0) + RELAX
    right = lines(1) + RELAX * params[2]
    parent = params[0]
    cond = params[1]
    place = lax.broadcasted_iota(jnp.int32, (nseg, width), 0).astype(jnp.float32)
    inverse = [None] * nseg
    hits = [None] * nseg
    for s in range(nseg - 1, 0, -1):
        c = cond[s : s + 1]
        e = excess[s : s + 1]
        inverse[s] = 1.0 / (e + c)
        ratio = c * inverse[s]
        hits[s] = place == parent[s : s + 1]
        excess = excess + jnp.where(hits[s], ratio * e, 0.0)
        right = right + jnp.where(hits[s], ratio * right[s : s + 1], 0.0)
    answer = jnp.where(place == 0.0, right[0:1] / excess[0:1], 0.0)
    for s in range(1, nseg):
        above = jnp.sum(jnp.where(hits[s], answer, 0.0), axis=0, keepdims=True)
        value = (right[s : s + 1] + cond[s : s + 1] * above) * inverse[s]
        answer = jnp.where(place == float(s), value, answer)
    for j in range(layers):
        solved[j] = answer[j * slab : (j + 1) * slab]
    mine = solved[layer]
    own_slab[...] = mine
    table[area] = mine
    back = []
    for d in range(1, groups):
        copy = pltpu.make_async_remote_copy(
            table.at[area], table.at[area], send_p.at[d], recv_p.at[d],
            device_id=areal_peer(d), device_id_type=MESH,
        )
        copy.start()
        back.append(copy)
    for copy in back:
        copy.wait_recv()
    for copy in halo:
        copy.wait()
    for copy in to_owner + to_layers + back:
        copy.wait_send()


def face_terms(geometry, left, right, kinds):
    trans = (geometry * 2.0) * (left[1] * right[1]) / (left[1] + right[1])
    drop = left[0] - right[0]
    if kinds is None:
        up = drop > 0
        flow = trans * drop
        return [flow * jnp.where(up, left[2][a], right[2][a]) for a in range(3)]
    out = []
    for a in range(3):
        potential = drop + kinds[a]
        out.append(trans * potential * jnp.where(potential > 0, left[2][a], right[2][a]))
    return out


def residual_kernel(
    slab, width, chunk, groups_count,
    flat_s, blocks_s, flat, seg, perf_press, perf_weight, table, press, sats, perm, before, after,
    old, pore, out, source, adds, lower,
):
    level = pl.program_id(0)
    depth, nx, ny = press.shape
    groups, slots = flat.shape

    @pl.when(level == 0)
    def _():
        source[...] = jnp.zeros_like(source)
        lower[...] = jnp.zeros_like(lower)
        target = panel_index(seg[...], slab, width)
        bins = lax.broadcasted_iota(jnp.int32, (slab * width, slots), 0)
        found = []
        for owner in range(groups):
            tab = table[owner]
            line = jnp.concatenate([tab[s : s + 1] for s in range(slab)], axis=1)
            left = jnp.concatenate(
                list(pieces(line)) + [jnp.zeros((5, slab * width), jnp.float32)], axis=0
            )
            hot = jnp.where(bins == target[owner : owner + 1], 1.0, 0.0).astype(jnp.bfloat16)
            value = jnp.dot(left.astype(jnp.bfloat16), hot, preferred_element_type=jnp.float32)
            found.append(value[0:1] + value[1:2] + value[2:3])
        rate = perf_weight[...] * (perf_press[...] - jnp.concatenate(found, axis=0))
        rate_t = jnp.transpose(tall(rate, LANES))
        lanes_t = jnp.transpose(tall(flat[...] % ny, LANES))
        lane = lax.broadcasted_iota(jnp.int32, (slots, ny), 1)
        for owner in range(groups):
            adds[owner * slots : (owner + 1) * slots, :] = jnp.where(
                lane == lanes_t[:, owner : owner + 1], rate_t[:, owner : owner + 1], 0.0
            )
        for owner in range(groups):
            for block in range(slots // BLOCK):
                base = owner * slots + block * BLOCK

                @pl.when(blocks_s[owner] > block)
                def _(base=base, owner=owner, block=block):
                    def step(i, carry):
                        for j in range(16):
                            at = i * 16 + j
                            number = flat_s[owner, block * BLOCK + at] // ny
                            row = pl.ds(number, 1)
                            source[row, :] = source[row, :] + adds[pl.ds(base + at, 1), :]
                        return carry

                    lax.fori_loop(0, BLOCK // 16, step, 0)

    area = lax.axis_index("areal")
    above = jnp.minimum(level + 1, depth - 1)
    inner = jnp.where(level + 1 < depth, GEOMETRY[0], 0.0)
    row_from = pl.multiple_of(level * nx, nx)

    def edge(halo, real):
        values = [halo[f, pl.ds(level, 1), :] for f in range(4)]
        return (values[0], jnp.where(real, values[3], 0.0), mobilities(values[1], values[2]))

    def line(x):
        return (
            press[level, x : x + 1, :],
            perm[level, x : x + 1, :],
            mobilities(sats[0, level, x : x + 1, :], sats[1, level, x : x + 1, :]),
        )

    carry = face_terms(GEOMETRY[1], edge(before, area > 0), line(0), None)
    column = lax.broadcasted_iota(jnp.int32, (chunk, ny), 1)
    for x in range(0, nx, chunk):
        span = slice(x, x + chunk)
        p = press[level, span, :]
        water = sats[0, level, span, :]
        gas_sat = sats[1, level, span, :]
        k = perm[level, span, :]
        lam = mobilities(water, gas_sat)
        here = (p, k, lam)
        beyond = line(x + chunk) if x + chunk < nx else edge(after, area < groups_count - 1)

        def shifted(value, row):
            return jnp.concatenate([value[1:], row], axis=0)

        there = (
            shifted(p, beyond[0]),
            shifted(k, beyond[1]),
            tuple(shifted(lam[a], beyond[2][a]) for a in range(3)),
        )
        flux = face_terms(GEOMETRY[1], here, there, None)
        total = []
        for a in range(3):
            total.append(flux[a] - jnp.concatenate([carry[a], flux[a][:-1]], axis=0))
        carry = [flux[a][chunk - 1 :] for a in range(3)]
        there = (
            pltpu.roll(p, ny - 1, 1),
            jnp.where(column < ny - 1, pltpu.roll(k, ny - 1, 1), 0.0),
            tuple(pltpu.roll(lam[a], ny - 1, 1) for a in range(3)),
        )
        flux = face_terms(GEOMETRY[2], here, there, None)
        for a in range(3):
            total[a] = total[a] + (flux[a] - pltpu.roll(flux[a], 1, 1))
        there = (
            press[above, span, :],
            perm[above, span, :],
            mobilities(sats[0, above, span, :], sats[1, above, span, :]),
        )
        flux = face_terms(inner, here, there, GRAVITY)
        well = source[pl.ds(row_from + x, chunk), :]
        volume = pore[0, span, :]
        old_water = old[0, 0, span, :]
        old_gas = old[1, 0, span, :]
        change = (
            water - old_water,
            (1.0 - water - gas_sat) - (1.0 - old_water - old_gas),
            gas_sat - old_gas,
        )
        for a in range(3):
            net = total[a] + (flux[a] - lower[a, span, :])
            lower[a, span, :] = flux[a]
            out[a, 0, span, :] = volume * change[a] + net + lam[a] * well


def ends_kernel(depth, given, press, sats, perm, below, over, out):
    rows = press.shape[1]
    chunk = 16
    end = pl.program_id(0)
    for x in range(0, rows, chunk):
        span = slice(x, x + chunk)
        here = (press[0, span, :], perm[0, span, :], mobilities(sats[0, 0, span, :], sats[1, 0, span, :]))

        def other(ref):
            return (ref[0, span, :], ref[3, span, :], mobilities(ref[1, span, :], ref[2, span, :]))

        @pl.when(end == 0)
        def _():
            flux = face_terms(GEOMETRY[0], other(below), here, GRAVITY)
            for a in range(3):
                out[a, 0, span, :] = given[a, 0, span, :] - flux[a]

        @pl.when(end == 1)
        def _():
            flux = face_terms(GEOMETRY[0], here, other(over), GRAVITY)
            for a in range(3):
                out[a, 0, span, :] = given[a, 0, span, :] + flux[a]


def on_device(
    pressure,
    saturations,
    old_saturations,
    permeability,
    pore_volume,
    perf_cell,
    perf_layer,
    perf_seg,
    perf_index,
    perf_blocks,
    seg_parent,
    seg_cond,
    seg_target,
):
    f32 = jnp.float32
    depth, nx, ny = pressure.shape
    groups, slots = perf_cell.shape[2:]
    layers = lax.axis_size("layer")
    wells, nseg = seg_parent.shape
    slab = nseg // layers
    width = -(-wells // LANES) * LANES
    halves = ny // LANES
    shape = jax.ShapeDtypeStruct
    vm = pl.BlockSpec(memory_space=VMEM)
    sm = pl.BlockSpec(memory_space=SMEM)

    up = [(i, i + 1) for i in range(layers - 1)]
    down = [(j, i) for i, j in up]
    top = jnp.concatenate([pressure[-1:], saturations[:, -1], permeability[-1:]], axis=0)
    bottom = jnp.concatenate([pressure[:1], saturations[:, 0], permeability[:1]], axis=0)
    below = lax.ppermute(top, "layer", up)
    over = lax.ppermute(bottom, "layer", down)

    flat = perf_layer[0, 0] * (nx * ny) + perf_cell[0, 0]
    seg = perf_seg[0, 0]
    count = perf_blocks[0, 0]
    tiles = 2 * slab * width // LANES
    sums, perf_press, perf_weight = pl.pallas_call(
        functools.partial(gather_kernel, slab, width, halves),
        out_shape=(
            shape((groups, tiles, LANES), f32),
            shape((groups, slots), f32),
            shape((groups, slots), f32),
        ),
        in_specs=[sm, sm] + [vm] * 6,
        out_specs=(vm, vm, vm),
        scratch_shapes=[VMEM((3, groups * slots, LANES), f32)],
        compiler_params=pltpu.CompilerParams(vmem_limit_bytes=VLIMIT),
        cost_estimate=pl.CostEstimate(flops=10**7, bytes_accessed=3 * 10**7, transcendentals=0),
        name="gather_perforations",
    )(
        flat, count, pressure.reshape(depth * nx, ny), saturations.reshape(2, depth * nx, ny),
        flat, seg, perf_index[0, 0], count[:, None],
    )

    params = jnp.stack([seg_parent.astype(f32), seg_cond, seg_target]).transpose(0, 2, 1)
    params = jnp.pad(params, ((0, 0), (0, 0), (0, width - wells)), constant_values=1.0)
    first = jnp.concatenate(
        [pressure[None, :, 0], saturations[:, :, 0], permeability[None, :, 0]], axis=0
    )
    last = jnp.concatenate(
        [pressure[None, :, -1], saturations[:, :, -1], permeability[None, :, -1]], axis=0
    )
    dma = pltpu.SemaphoreType.DMA
    table, own_slab, before, after = pl.pallas_call(
        functools.partial(wells_kernel, groups, layers, slab, width),
        out_shape=(
            shape((groups, slab, width), f32),
            shape((slab, width), f32),
            shape(first.shape, f32),
            shape(first.shape, f32),
        ),
        in_specs=[vm] * 4,
        out_specs=(vm,) * 4,
        scratch_shapes=[
            VMEM((groups, tiles, LANES), f32),
            VMEM((layers, tiles, LANES), f32),
            VMEM((layers, slab, width), f32),
            dma((groups,)), dma((groups,)),
            dma((layers,)), dma((layers,)),
            dma((groups,)), dma((groups,)),
            dma((2,)), dma((2,)),
        ],
        compiler_params=pltpu.CompilerParams(collective_id=0, has_side_effects=True),
        cost_estimate=pl.CostEstimate(flops=10**6, bytes_accessed=10**7, transcendentals=0),
        name="solve_wells",
    )(sums, params, first, last)

    plane = lambda n: pl.BlockSpec((n, 1, nx, ny), lambda i: (0, i, 0, 0))
    residual = pl.pallas_call(
        functools.partial(residual_kernel, slab, width, 16, groups),
        grid=(depth,),
        out_shape=shape((3, depth, nx, ny), f32),
        in_specs=[sm, sm] + [vm] * 10 + [plane(2), pl.BlockSpec((1, nx, ny), lambda i: (i, 0, 0))],
        out_specs=plane(3),
        scratch_shapes=[
            VMEM((depth * nx, ny), f32),
            VMEM((groups * slots, ny), f32),
            VMEM((3, nx, ny), f32),
        ],
        compiler_params=pltpu.CompilerParams(
            vmem_limit_bytes=VLIMIT, dimension_semantics=("arbitrary",)
        ),
        cost_estimate=pl.CostEstimate(flops=10**8, bytes_accessed=6 * 10**7, transcendentals=0),
        name="cell_residual",
    )(
        flat, count, flat, seg, perf_press, perf_weight, table,
        pressure, saturations, permeability, before, after, old_saturations, pore_volume,
    )

    part = 64 if nx % 64 == 0 else nx
    ends = lambda n: pl.BlockSpec((n, 1, part, ny), lambda e, j: (0, e * (depth - 1), j, 0))
    flat_end = pl.BlockSpec((1, part, ny), lambda e, j: (e * (depth - 1), j, 0))
    halo = pl.BlockSpec((4, part, ny), lambda e, j: (0, j, 0))
    residual = pl.pallas_call(
        functools.partial(ends_kernel, depth),
        grid=(2, nx // part),
        out_shape=shape(residual.shape, f32),
        in_specs=[ends(3), flat_end, ends(2), flat_end, halo, halo],
        out_specs=ends(3),
        input_output_aliases={0: 0},
        compiler_params=pltpu.CompilerParams(dimension_semantics=("arbitrary", "arbitrary")),
        cost_estimate=pl.CostEstimate(flops=10**7, bytes_accessed=8 * 10**6, transcendentals=0),
        name="outer_layers",
    )(residual, pressure, saturations, permeability, below, over)
    return residual, own_slab[:, :wells].T


def solution(mesh):
    return jax.shard_map(
        on_device,
        mesh=mesh,
        in_specs=(
            P("layer", "areal", None),
            P(None, "layer", "areal", None),
            P(None, "layer", "areal", None),
            P("layer", "areal", None),
            P("layer", "areal", None),
            P("layer", "areal", None, None),
            P("layer", "areal", None, None),
            P("layer", "areal", None, None),
            P("layer", "areal", None, None),
            P("layer", "areal", None),
            P("areal", None),
            P("areal", None),
            P("areal", None),
        ),
        out_specs=(P(None, "layer", "areal", None), P("areal", "layer")),
        check_vma=False,
    )
```

```python
import functools

import jax
import jax.numpy as jnp
from jax import lax
from jax.experimental import pallas as pl
from jax.experimental.pallas import tpu as pltpu
from jax.sharding import PartitionSpec as P

BLOCK = 128
LANES = 128

MU_WATER = 0.5
MU_OIL = 2.0
MU_GAS = 0.2
GRAVITY = (0.35, 0.28, 0.07)
GEOMETRY = (0.4, 1.0, 1.0)
RELAX = 20.0

VMEM = pltpu.VMEM
SMEM = pltpu.SMEM
MESH = pl.DeviceIdType.MESH
VLIMIT = 56 * 1024 * 1024


def mobilities(water, gas_sat):
    oil_sat = 1.0 - water - gas_sat
    return (
        water * water * (1.0 / MU_WATER),
        oil_sat * oil_sat * (1.0 / MU_OIL),
        gas_sat * gas_sat * (1.0 / MU_GAS),
    )


def pieces(value):
    high = value.astype(jnp.bfloat16).astype(jnp.float32)
    rest = value - high
    mid = rest.astype(jnp.bfloat16).astype(jnp.float32)
    return high, mid, rest - mid


def panel_index(seg, slab, width):
    return (seg % slab) * width + seg // slab


def tall(value, rows):
    return jnp.concatenate(
        [value, jnp.zeros((rows - value.shape[0], value.shape[1]), value.dtype)], axis=0
    )


def split(value, size):
    if size & (size - 1) == 0:
        return lax.shift_right_logical(value, size.bit_length() - 1), value & (size - 1)
    return value // size, value % size


def column_part(row, part, halves):
    value = row[:, :LANES]
    for h in range(1, halves):
        value = jnp.where(part == h, row[:, h * LANES : (h + 1) * LANES], value)
    return value


def gather_kernel(
    slab, width, halves, flat_s, blocks_s, press, sats, flat, seg, index, blocks,
    sums, perf_press, perf_weight, rows,
):
    groups, slots = flat.shape
    for owner in range(groups):
        for block in range(slots // BLOCK):
            base = owner * slots + block * BLOCK

            @pl.when(blocks_s[owner] > block)
            def _(base=base, owner=owner, block=block):
                def step(i, carry):
                    for j in range(16):
                        at = i * 16 + j
                        number, column = split(flat_s[owner, block * BLOCK + at], halves * LANES)
                        row = pl.ds(number, 1)
                        part = split(column, LANES)[0]
                        here = pl.ds(base + at, 1)
                        rows[0, here, :] = column_part(press[row, :], part, halves)
                        rows[1, here, :] = column_part(sats[0, row, :], part, halves)
                        rows[2, here, :] = column_part(sats[1, row, :], part, halves)
                    return carry

                lax.fori_loop(0, BLOCK // 16, step, 0)

    lanes_t = jnp.transpose(tall(flat[...] % LANES, LANES))
    lane = lax.broadcasted_iota(jnp.int32, (slots, LANES), 1)
    picked = jnp.zeros((slots, LANES), jnp.float32)
    for owner in range(groups):
        mask = lane == lanes_t[:, owner : owner + 1]
        for field in range(3):
            row = rows[field, owner * slots : (owner + 1) * slots, :]
            value = jnp.sum(jnp.where(mask, row, 0.0), axis=1, keepdims=True)
            picked = jnp.where(lane == field * groups + owner, value, picked)
    picked = jnp.transpose(picked)
    live = lax.broadcasted_iota(jnp.int32, (groups, slots), 1) < blocks[...] * BLOCK
    pressure = jnp.where(live, picked[0:groups], 0.0)
    water = picked[groups : 2 * groups]
    gas_sat = picked[2 * groups : 3 * groups]
    weight = jnp.where(live, index[...], 0.0)
    lam = mobilities(water, gas_sat)
    mobile = jnp.where(live, weight * lam[0] + weight * lam[1] + weight * lam[2], 0.0)
    perf_press[...] = pressure
    perf_weight[...] = weight
    parts = pieces(mobile) + pieces(mobile * pressure)
    target = panel_index(seg[...], slab, width)
    bins = lax.broadcasted_iota(jnp.int32, (slab * width, slots), 0)
    zero = jnp.zeros((2, slots), jnp.float32)
    chunks = slab * width // LANES
    for owner in range(groups):
        left = jnp.concatenate([part[owner : owner + 1] for part in parts] + [zero], axis=0)
        hot = jnp.where(bins == target[owner : owner + 1], 1.0, 0.0).astype(jnp.bfloat16)
        total = lax.dot_general(
            left.astype(jnp.bfloat16), hot, (((1,), (1,)), ((), ())),
            preferred_element_type=jnp.float32,
        )
        for kind in range(2):
            line = total[3 * kind : 3 * kind + 1] + total[3 * kind + 1 : 3 * kind + 2]
            line = line + total[3 * kind + 2 : 3 * kind + 3]
            for c in range(chunks):
                sums[owner, kind * chunks + c : kind * chunks + c + 1, :] = line[
                    :, c * LANES : (c + 1) * LANES
                ]


def face_terms(geometry, left, right, kinds):
    trans = (geometry * 2.0) * (left[1] * right[1]) / (left[1] + right[1])
    drop = left[0] - right[0]
    if kinds is None:
        up = drop > 0
        flow = trans * drop
        return [flow * jnp.where(up, left[2][a], right[2][a]) for a in range(3)]
    out = []
    for a in range(3):
        potential = drop + kinds[a]
        out.append(trans * potential * jnp.where(potential > 0, left[2][a], right[2][a]))
    return out


def flow_kernel(
    groups, layers, slab, width, chunk, sums, params, press, sats, perm, old, pore,
    out, below, over, table, own_slab, edges,
    got, panel, solved, back, rims, halos, lower,
    send_a, recv_a, send_l, recv_l, send_p, recv_p, send_x, recv_x, send_z, recv_z,
):
    level = pl.program_id(0)
    depth, nx, ny = press.shape
    area = lax.axis_index("areal")
    layer = lax.axis_index("layer")
    nseg = layers * slab
    half = width // LANES

    def areal_peer(d):
        return {"areal": lax.rem(area + d, groups)}

    def layer_peer(d):
        return {"layer": lax.rem(layer + d, layers)}

    def remote(source, target, send, recv, peer):
        return pltpu.make_async_remote_copy(
            source, target, send, recv, device_id=peer, device_id_type=MESH
        )

    def to_owner(d):
        return remote(
            sums.at[lax.rem(area + d, groups)], got.at[d], send_a.at[d], recv_a.at[d], areal_peer(d)
        )

    def to_layer(d):
        return remote(
            panel.at[layer], panel.at[layer], send_l.at[d], recv_l.at[d], layer_peer(d)
        )

    def to_source(d):
        return remote(back.at[area], back.at[area], send_p.at[d], recv_p.at[d], areal_peer(d))

    def rim(side):
        return remote(
            rims.at[side], halos.at[side], send_x.at[side], recv_x.at[side],
            areal_peer(groups - 1 if side else 1),
        )

    def planes(side):
        at = 0 if side else depth - 1
        target = over if side else below
        peer = layer_peer(layers - 1 if side else 1)
        fields = (press.at[at], sats.at[0, at], sats.at[1, at], perm.at[at])
        return [
            remote(fields[f], target.at[f], send_z.at[side, f], recv_z.at[side, f], peer)
            for f in range(4)
        ]

    @pl.when(level == 0)
    def _():
        barrier = pltpu.get_barrier_semaphore()
        for d in range(1, groups):
            pl.semaphore_signal(barrier, inc=1, device_id=areal_peer(d), device_id_type=MESH)
        for d in range(1, layers):
            pl.semaphore_signal(barrier, inc=1, device_id=layer_peer(d), device_id_type=MESH)
        for side in range(2):
            row = slice(0, 1) if side else slice(nx - 1, nx)
            for i in range(depth):
                for f, value in enumerate(
                    (press[i, row, :], sats[0, i, row, :], sats[1, i, row, :], perm[i, row, :])
                ):
                    rims[side, f, i : i + 1, :] = value
        lower[...] = jnp.zeros_like(lower)
        pl.semaphore_wait(barrier, groups + layers - 2)
        for d in range(1, groups):
            to_owner(d).start()
        for side in range(2):
            rim(side).start()

        @pl.when(layer < layers - 1)
        def _():
            for copy in planes(0):
                copy.start()

        @pl.when(layer > 0)
        def _():
            for copy in planes(1):
                copy.start()

    @pl.when(level == 1)
    def _():
        total = sums[area]
        for d in range(1, groups):
            to_owner(d).wait_recv()
            total = total + got[d]
        panel[layer] = total
        for d in range(1, layers):
            to_layer(d).start()

    @pl.when(level == depth - 2)
    def _():
        for d in range(1, layers):
            remote(
                panel.at[layer], panel.at[lax.rem(layer + layers - d, layers)],
                send_l.at[d], recv_l.at[d], layer_peer(d),
            ).wait_recv()

        def lines(kind):
            result = []
            for j in range(layers):
                tile = panel[j]
                for s in range(slab):
                    at = (kind * slab + s) * half
                    result.append(
                        jnp.concatenate([tile[at + h : at + h + 1] for h in range(half)], axis=1)
                    )
            return jnp.concatenate(result, axis=0)

        excess = lines(0) + RELAX
        right = lines(1) + RELAX * params[2]
        parent = params[0]
        cond = params[1]
        place = lax.broadcasted_iota(jnp.int32, (nseg, width), 0).astype(jnp.float32)
        inverse = [None] * nseg
        hits = [None] * nseg
        for s in range(nseg - 1, 0, -1):
            c = cond[s : s + 1]
            e = excess[s : s + 1]
            inverse[s] = 1.0 / (e + c)
            ratio = c * inverse[s]
            hits[s] = place == parent[s : s + 1]
            excess = excess + jnp.where(hits[s], ratio * e, 0.0)
            right = right + jnp.where(hits[s], ratio * right[s : s + 1], 0.0)
        answer = jnp.where(place == 0.0, right[0:1] / excess[0:1], 0.0)
        for s in range(1, nseg):
            above = jnp.sum(jnp.where(hits[s], answer, 0.0), axis=0, keepdims=True)
            value = (right[s : s + 1] + cond[s : s + 1] * above) * inverse[s]
            answer = jnp.where(place == float(s), value, answer)
        for j in range(layers):
            solved[j] = answer[j * slab : (j + 1) * slab]
        back[area] = solved[layer]
        for d in range(1, groups):
            to_source(d).start()

    above = jnp.minimum(level + 1, depth - 1)
    inner = jnp.where(level + 1 < depth, GEOMETRY[0], 0.0)
    carry = [jnp.zeros((1, ny), jnp.float32)] * 3
    column = lax.broadcasted_iota(jnp.int32, (chunk, ny), 1)
    for x in range(0, nx, chunk):
        span = slice(x, x + chunk)
        p = press[level, span, :]
        water = sats[0, level, span, :]
        gas_sat = sats[1, level, span, :]
        k = perm[level, span, :]
        lam = mobilities(water, gas_sat)
        here = (p, k, lam)
        y = min(x + chunk, nx - 1)
        row = slice(y, y + 1)
        next_k = perm[level, row, :] if x + chunk < nx else jnp.zeros((1, ny), jnp.float32)
        next_lam = mobilities(sats[0, level, row, :], sats[1, level, row, :])

        def shifted(value, end):
            return jnp.concatenate([value[1:], end], axis=0)

        there = (
            shifted(p, press[level, row, :]),
            shifted(k, next_k),
            tuple(shifted(lam[a], next_lam[a]) for a in range(3)),
        )
        flux = face_terms(GEOMETRY[1], here, there, None)
        total = []
        for a in range(3):
            total.append(flux[a] - jnp.concatenate([carry[a], flux[a][:-1]], axis=0))
        carry = [flux[a][chunk - 1 :] for a in range(3)]
        there = (
            pltpu.roll(p, ny - 1, 1),
            jnp.where(column < ny - 1, pltpu.roll(k, ny - 1, 1), 0.0),
            tuple(pltpu.roll(lam[a], ny - 1, 1) for a in range(3)),
        )
        flux = face_terms(GEOMETRY[2], here, there, None)
        for a in range(3):
            total[a] = total[a] + (flux[a] - pltpu.roll(flux[a], 1, 1))
        there = (
            press[above, span, :],
            perm[above, span, :],
            mobilities(sats[0, above, span, :], sats[1, above, span, :]),
        )
        flux = face_terms(inner, here, there, GRAVITY)
        volume = pore[0, span, :]
        old_water = old[0, 0, span, :]
        old_gas = old[1, 0, span, :]
        change = (
            water - old_water,
            (1.0 - water - gas_sat) - (1.0 - old_water - old_gas),
            gas_sat - old_gas,
        )
        for a in range(3):
            net = total[a] + (flux[a] - lower[a, span, :])
            lower[a, span, :] = flux[a]
            out[a, 0, span, :] = volume * change[a] + net

    @pl.when(level == depth - 1)
    def _():
        for side in range(2):
            rim(side).wait()

        def side_of(ref, side):
            return (
                ref[side, 0], ref[side, 3], mobilities(ref[side, 1], ref[side, 2])
            )

        low = face_terms(GEOMETRY[1], side_of(halos, 0), side_of(rims, 1), None)
        high = face_terms(GEOMETRY[1], side_of(rims, 0), side_of(halos, 1), None)
        for a in range(3):
            edges[a] = jnp.where(area > 0, low[a], 0.0)
            edges[3 + a] = jnp.where(area < groups - 1, high[a], 0.0)
        for d in range(1, groups):
            remote(
                back.at[area], back.at[lax.rem(area + groups - d, groups)],
                send_p.at[d], recv_p.at[d], areal_peer(d),
            ).wait_recv()
        table[...] = back[...]
        own_slab[...] = solved[layer]
        for d in range(1, groups):
            to_owner(d).wait_send()
            to_source(d).wait_send()
        for d in range(1, layers):
            to_layer(d).wait_send()

        @pl.when(layer < layers - 1)
        def _():
            for copy in planes(0):
                copy.wait_send()
            for copy in planes(1):
                copy.wait_recv()

        @pl.when(layer > 0)
        def _():
            for copy in planes(1):
                copy.wait_send()
            for copy in planes(0):
                copy.wait_recv()


def finish_kernel(
    slab, width, chunk, layers,
    flat_s, blocks_s, flat, seg, perf_press, perf_weight, table, edges, below, over,
    base_in, sats, press, perm, out, source, source_b, adds,
):
    level = pl.program_id(0)
    depth = pl.num_programs(0)
    nx, ny = press.shape[1:]
    groups, slots = flat.shape
    layer = lax.axis_index("layer")

    @pl.when(level == 0)
    def _():
        source[...] = jnp.zeros_like(source)
        source_b[...] = jnp.zeros_like(source_b)
        target = panel_index(seg[...], slab, width)
        bins = lax.broadcasted_iota(jnp.int32, (slab * width, slots), 0)
        found = []
        for owner in range(groups):
            tab = table[owner]
            line = jnp.concatenate([tab[s : s + 1] for s in range(slab)], axis=1)
            left = jnp.concatenate(
                list(pieces(line)) + [jnp.zeros((5, slab * width), jnp.float32)], axis=0
            )
            hot = jnp.where(bins == target[owner : owner + 1], 1.0, 0.0).astype(jnp.bfloat16)
            value = jnp.dot(left.astype(jnp.bfloat16), hot, preferred_element_type=jnp.float32)
            found.append(value[0:1] + value[1:2] + value[2:3])
        rate = perf_weight[...] * (perf_press[...] - jnp.concatenate(found, axis=0))
        rate_t = jnp.transpose(tall(rate, LANES))
        lanes_t = jnp.transpose(tall(flat[...] % ny, LANES))
        lane = lax.broadcasted_iota(jnp.int32, (slots, ny), 1)
        for owner in range(groups):
            adds[owner * slots : (owner + 1) * slots, :] = jnp.where(
                lane == lanes_t[:, owner : owner + 1], rate_t[:, owner : owner + 1], 0.0
            )
        for owner in range(groups):
            for block in range(slots // BLOCK):
                base = owner * slots + block * BLOCK

                @pl.when(blocks_s[owner] > block)
                def _(base=base, owner=owner, block=block):
                    def step(i, carry):
                        for j in range(16):
                            at = i * 16 + j
                            number = split(flat_s[owner, block * BLOCK + at], ny)[0]
                            row = pl.ds(number, 1)
                            into = source if j % 2 == 0 else source_b
                            into[row, :] = into[row, :] + adds[pl.ds(base + at, 1), :]
                        return carry

                    lax.fori_loop(0, BLOCK // 16, step, 0)

    row_from = pl.multiple_of(level * nx, nx)
    for x in range(0, nx, chunk):
        span = slice(x, x + chunk)
        lam = mobilities(sats[0, 0, span, :], sats[1, 0, span, :])
        rows = pl.ds(row_from + x, chunk)
        well = source[rows, :] + source_b[rows, :]
        for a in range(3):
            out[a, 0, span, :] = base_in[a, 0, span, :] + lam[a] * well
    for a in range(3):
        out[a, 0, 0:1, :] = out[a, 0, 0:1, :] - edges[a, pl.ds(level, 1), :]
        out[a, 0, nx - 1 : nx, :] = out[a, 0, nx - 1 : nx, :] + edges[3 + a, pl.ds(level, 1), :]

    def ends(halo, real, sign):
        for x in range(0, nx, chunk):
            span = slice(x, x + chunk)
            here = (press[0, span, :], perm[0, span, :], mobilities(sats[0, 0, span, :], sats[1, 0, span, :]))
            there = (halo[0, span, :], halo[3, span, :], mobilities(halo[1, span, :], halo[2, span, :]))
            pair = (here, there) if sign > 0 else (there, here)
            flux = face_terms(GEOMETRY[0], pair[0], pair[1], GRAVITY)
            for a in range(3):
                out[a, 0, span, :] = out[a, 0, span, :] + sign * jnp.where(real, flux[a], 0.0)

    @pl.when(level == 0)
    def _():
        ends(below, layer > 0, -1.0)

    @pl.when(level == depth - 1)
    def _():
        ends(over, layer < layers - 1, 1.0)


def on_device(
    pressure,
    saturations,
    old_saturations,
    permeability,
    pore_volume,
    perf_cell,
    perf_layer,
    perf_seg,
    perf_index,
    perf_blocks,
    seg_parent,
    seg_cond,
    seg_target,
):
    f32 = jnp.float32
    depth, nx, ny = pressure.shape
    groups, slots = perf_cell.shape[2:]
    layers = lax.axis_size("layer")
    wells, nseg = seg_parent.shape
    slab = nseg // layers
    width = -(-wells // LANES) * LANES
    halves = ny // LANES
    shape = jax.ShapeDtypeStruct
    vm = pl.BlockSpec(memory_space=VMEM)
    sm = pl.BlockSpec(memory_space=SMEM)

    flat = perf_layer[0, 0] * (nx * ny) + perf_cell[0, 0]
    seg = perf_seg[0, 0]
    count = perf_blocks[0, 0]
    tiles = 2 * slab * width // LANES
    sums, perf_press, perf_weight = pl.pallas_call(
        functools.partial(gather_kernel, slab, width, halves),
        out_shape=(
            shape((groups, tiles, LANES), f32),
            shape((groups, slots), f32),
            shape((groups, slots), f32),
        ),
        in_specs=[sm, sm] + [vm] * 6,
        out_specs=(vm, vm, vm),
        scratch_shapes=[VMEM((3, groups * slots, LANES), f32)],
        compiler_params=pltpu.CompilerParams(vmem_limit_bytes=VLIMIT),
        cost_estimate=pl.CostEstimate(flops=10**7, bytes_accessed=3 * 10**7, transcendentals=0),
        name="gather_perforations",
    )(
        flat, count, pressure.reshape(depth * nx, ny), saturations.reshape(2, depth * nx, ny),
        flat, seg, perf_index[0, 0], count[:, None],
    )

    params = jnp.stack([seg_parent.astype(f32), seg_cond, seg_target]).transpose(0, 2, 1)
    params = jnp.pad(params, ((0, 0), (0, 0), (0, width - wells)), constant_values=1.0)
    dma = pltpu.SemaphoreType.DMA
    anywhere = pl.BlockSpec(memory_space=pl.ANY)
    plane = lambda n: pl.BlockSpec((n, 1, nx, ny), lambda i: (0, i, 0, 0))
    arbitrary = ("arbitrary",)
    base, below, over, table, own_slab, edges = pl.pallas_call(
        functools.partial(flow_kernel, groups, layers, slab, width, 16),
        grid=(depth,),
        out_shape=(
            shape((3, depth, nx, ny), f32),
            shape((4, nx, ny), f32),
            shape((4, nx, ny), f32),
            shape((groups, slab, width), f32),
            shape((slab, width), f32),
            shape((6, depth, ny), f32),
        ),
        in_specs=[vm] * 5 + [plane(2), pl.BlockSpec((1, nx, ny), lambda i: (i, 0, 0))],
        out_specs=(plane(3), anywhere, anywhere, vm, vm, vm),
        scratch_shapes=[
            VMEM((groups, tiles, LANES), f32),
            VMEM((layers, tiles, LANES), f32),
            VMEM((layers, slab, width), f32),
            VMEM((groups, slab, width), f32),
            VMEM((2, 4, depth, ny), f32),
            VMEM((2, 4, depth, ny), f32),
            VMEM((3, nx, ny), f32),
            dma((groups,)), dma((groups,)),
            dma((layers,)), dma((layers,)),
            dma((groups,)), dma((groups,)),
            dma((2,)), dma((2,)),
            dma((2, 4)), dma((2, 4)),
        ],
        compiler_params=pltpu.CompilerParams(
            collective_id=0, has_side_effects=True,
            vmem_limit_bytes=VLIMIT, dimension_semantics=arbitrary,
        ),
        cost_estimate=pl.CostEstimate(flops=10**8, bytes_accessed=6 * 10**7, transcendentals=0),
        name="block_flow",
    )(sums, params, pressure, saturations, permeability, old_saturations, pore_volume)

    end_plane = pl.BlockSpec((1, nx, ny), lambda i: (jnp.where(i == depth - 1, i, 0), 0, 0))
    residual = pl.pallas_call(
        functools.partial(finish_kernel, slab, width, 16, layers),
        grid=(depth,),
        out_shape=shape((3, depth, nx, ny), f32),
        in_specs=[sm, sm] + [vm] * 8 + [plane(3), plane(2), end_plane, end_plane],
        out_specs=plane(3),
        scratch_shapes=[
            VMEM((depth * nx, ny), f32),
            VMEM((depth * nx, ny), f32),
            VMEM((groups * slots, ny), f32),
        ],
        compiler_params=pltpu.CompilerParams(
            vmem_limit_bytes=VLIMIT, dimension_semantics=arbitrary
        ),
        cost_estimate=pl.CostEstimate(flops=10**7, bytes_accessed=2 * 10**7, transcendentals=0),
        name="wells_and_ends",
    )(
        flat, count, flat, seg, perf_press, perf_weight, table, edges, below, over,
        base, saturations, pressure, permeability,
    )
    return residual, own_slab[:, :wells].T


def solution(mesh):
    return jax.shard_map(
        on_device,
        mesh=mesh,
        in_specs=(
            P("layer", "areal", None),
            P(None, "layer", "areal", None),
            P(None, "layer", "areal", None),
            P("layer", "areal", None),
            P("layer", "areal", None),
            P("layer", "areal", None, None),
            P("layer", "areal", None, None),
            P("layer", "areal", None, None),
            P("layer", "areal", None, None),
            P("layer", "areal", None),
            P("areal", None),
            P("areal", None),
            P("areal", None),
        ),
        out_specs=(P(None, "layer", "areal", None), P("areal", "layer")),
        check_vma=False,
    )
```

```python
import functools

import jax
import jax.numpy as jnp
from jax import lax
from jax.experimental import pallas as pl
from jax.experimental.pallas import tpu as pltpu
from jax.sharding import PartitionSpec as P

BLOCK = 128
LANES = 128

MU_WATER = 0.5
MU_OIL = 2.0
MU_GAS = 0.2
GRAVITY = (0.35, 0.28, 0.07)
GEOMETRY = (0.4, 1.0, 1.0)
RELAX = 20.0

VMEM = pltpu.VMEM
SMEM = pltpu.SMEM
MESH = pl.DeviceIdType.MESH
VLIMIT = 56 * 1024 * 1024


def mobilities(water, gas_sat):
    oil_sat = 1.0 - water - gas_sat
    return (
        water * water * (1.0 / MU_WATER),
        oil_sat * oil_sat * (1.0 / MU_OIL),
        gas_sat * gas_sat * (1.0 / MU_GAS),
    )


def pieces(value):
    high = value.astype(jnp.bfloat16).astype(jnp.float32)
    rest = value - high
    mid = rest.astype(jnp.bfloat16).astype(jnp.float32)
    return high, mid, rest - mid


def panel_index(seg, slab, width):
    return (seg % slab) * width + seg // slab


def tall(value, rows):
    return jnp.concatenate(
        [value, jnp.zeros((rows - value.shape[0], value.shape[1]), value.dtype)], axis=0
    )


def split(value, size):
    if size & (size - 1) == 0:
        return lax.shift_right_logical(value, size.bit_length() - 1), value & (size - 1)
    return value // size, value % size


def column_part(row, part, halves):
    value = row[:, :LANES]
    for h in range(1, halves):
        value = jnp.where(part == h, row[:, h * LANES : (h + 1) * LANES], value)
    return value


def gather_kernel(
    slab, width, halves, flat_s, blocks_s, press, sats, flat, seg, index,
    sums, perf_press, perf_weight, rows,
):
    groups, slots = flat.shape
    for owner in range(groups):
        for block in range(slots // BLOCK):
            base = owner * slots + block * BLOCK

            @pl.when(blocks_s[owner] > block)
            def _(base=base, owner=owner, block=block):
                def step(i, carry):
                    for j in range(16):
                        at = i * 16 + j
                        number, column = split(flat_s[owner, block * BLOCK + at], halves * LANES)
                        row = pl.ds(number, 1)
                        part = split(column, LANES)[0]
                        here = pl.ds(base + at, 1)
                        rows[0, here, :] = column_part(press[row, :], part, halves)
                        rows[1, here, :] = column_part(sats[0, row, :], part, halves)
                        rows[2, here, :] = column_part(sats[1, row, :], part, halves)
                    return carry

                lax.fori_loop(0, BLOCK // 16, step, 0)

    lanes_t = jnp.transpose(tall(flat[...] % LANES, LANES))
    lane = lax.broadcasted_iota(jnp.int32, (slots, LANES), 1)
    picked = jnp.zeros((slots, LANES), jnp.float32)
    for owner in range(groups):
        mask = lane == lanes_t[:, owner : owner + 1]
        for field in range(3):
            row = rows[field, owner * slots : (owner + 1) * slots, :]
            value = jnp.sum(jnp.where(mask, row, 0.0), axis=1, keepdims=True)
            picked = jnp.where(lane == field * groups + owner, value, picked)
    picked = jnp.transpose(picked)
    owners = lax.broadcasted_iota(jnp.int32, (groups, slots), 0)
    limit = jnp.zeros((groups, slots), jnp.int32)
    for owner in range(groups):
        limit = jnp.where(owners == owner, blocks_s[owner] * BLOCK, limit)
    live = lax.broadcasted_iota(jnp.int32, (groups, slots), 1) < limit
    pressure = jnp.where(live, picked[0:groups], 0.0)
    water = picked[groups : 2 * groups]
    gas_sat = picked[2 * groups : 3 * groups]
    weight = jnp.where(live, index[...], 0.0)
    lam = mobilities(water, gas_sat)
    mobile = jnp.where(live, weight * lam[0] + weight * lam[1] + weight * lam[2], 0.0)
    perf_press[...] = pressure
    perf_weight[...] = weight
    parts = pieces(mobile) + pieces(mobile * pressure)
    target = panel_index(seg[...], slab, width)
    bins = lax.broadcasted_iota(jnp.int32, (slab * width, slots), 0)
    zero = jnp.zeros((2, slots), jnp.float32)
    chunks = slab * width // LANES
    for owner in range(groups):
        left = jnp.concatenate([part[owner : owner + 1] for part in parts] + [zero], axis=0)
        hot = jnp.where(bins == target[owner : owner + 1], 1.0, 0.0).astype(jnp.bfloat16)
        total = lax.dot_general(
            left.astype(jnp.bfloat16), hot, (((1,), (1,)), ((), ())),
            preferred_element_type=jnp.float32,
        )
        for kind in range(2):
            line = total[3 * kind : 3 * kind + 1] + total[3 * kind + 1 : 3 * kind + 2]
            line = line + total[3 * kind + 2 : 3 * kind + 3]
            for c in range(chunks):
                sums[owner, kind * chunks + c : kind * chunks + c + 1, :] = line[
                    :, c * LANES : (c + 1) * LANES
                ]


def face_terms(geometry, left, right, kinds):
    trans = (geometry * 2.0) * (left[1] * right[1]) / (left[1] + right[1])
    drop = left[0] - right[0]
    if kinds is None:
        up = drop > 0
        flow = trans * drop
        return [flow * jnp.where(up, left[2][a], right[2][a]) for a in range(3)]
    out = []
    for a in range(3):
        potential = drop + kinds[a]
        out.append(trans * potential * jnp.where(potential > 0, left[2][a], right[2][a]))
    return out


def flow_kernel(
    groups, layers, slab, width, chunk, sums, seg_parent, seg_cond, seg_target, press, sats, perm, old, pore,
    out, below, over, table, own_slab, edges,
    got, panel, solved, back, rims, halos, lower, wide, wide_parent,
    send_a, recv_a, send_l, recv_l, send_p, recv_p, send_x, recv_x, send_z, recv_z,
):
    level = pl.program_id(0)
    depth, nx, ny = press.shape
    area = lax.axis_index("areal")
    layer = lax.axis_index("layer")
    nseg = layers * slab
    half = width // LANES

    def areal_peer(d):
        return {"areal": lax.rem(area + d, groups)}

    def layer_peer(d):
        return {"layer": lax.rem(layer + d, layers)}

    def remote(source, target, send, recv, peer):
        return pltpu.make_async_remote_copy(
            source, target, send, recv, device_id=peer, device_id_type=MESH
        )

    def to_owner(d):
        return remote(
            sums.at[lax.rem(area + d, groups)], got.at[d], send_a.at[d], recv_a.at[d], areal_peer(d)
        )

    def to_layer(d):
        return remote(
            panel.at[layer], panel.at[layer], send_l.at[d], recv_l.at[d], layer_peer(d)
        )

    def to_source(d):
        return remote(back.at[area], back.at[area], send_p.at[d], recv_p.at[d], areal_peer(d))

    def rim(side):
        return remote(
            rims.at[side], halos.at[side], send_x.at[side], recv_x.at[side],
            areal_peer(groups - 1 if side else 1),
        )

    def planes(side, fields_of=range(4)):
        at = 0 if side else depth - 1
        target = over if side else below
        peer = layer_peer(layers - 1 if side else 1)
        fields = (press.at[at], sats.at[0, at], sats.at[1, at], perm.at[at])
        return [
            remote(fields[f], target.at[f], send_z.at[side, f], recv_z.at[side, f], peer)
            for f in fields_of
        ]

    def start_planes(fields_of):
        @pl.when(layer < layers - 1)
        def _():
            for copy in planes(0, fields_of):
                copy.start()

        @pl.when(layer > 0)
        def _():
            for copy in planes(1, fields_of):
                copy.start()

    @pl.when(level == 0)
    def _():
        barrier = pltpu.get_barrier_semaphore()
        for d in range(1, groups):
            pl.semaphore_signal(barrier, inc=1, device_id=areal_peer(d), device_id_type=MESH)
        for d in range(1, layers):
            pl.semaphore_signal(barrier, inc=1, device_id=layer_peer(d), device_id_type=MESH)
        for side in range(2):
            row = slice(0, 1) if side else slice(nx - 1, nx)
            for i in range(depth):
                for f, value in enumerate(
                    (press[i, row, :], sats[0, i, row, :], sats[1, i, row, :], perm[i, row, :])
                ):
                    rims[side, f, i : i + 1, :] = value
        lower[...] = jnp.zeros_like(lower)
        pl.semaphore_wait(barrier, groups + layers - 2)
        for d in range(1, groups):
            to_owner(d).start()
        for side in range(2):
            rim(side).start()
        start_planes((0, 1))

    @pl.when(level == 1)
    def _():
        total = sums[area]
        for d in range(1, groups):
            to_owner(d).wait_recv()
            total = total + got[d]
        panel[layer] = total
        for d in range(1, layers):
            to_layer(d).start()
        start_planes((2, 3))

    @pl.when(level == depth - 2)
    def _():
        for d in range(1, layers):
            remote(
                panel.at[layer], panel.at[lax.rem(layer + layers - d, layers)],
                send_l.at[d], recv_l.at[d], layer_peer(d),
            ).wait_recv()

        def lines(kind):
            result = []
            for j in range(layers):
                tile = panel[j]
                for s in range(slab):
                    at = (kind * slab + s) * half
                    result.append(
                        jnp.concatenate([tile[at + h : at + h + 1] for h in range(half)], axis=1)
                    )
            return jnp.concatenate(result, axis=0)

        excess = lines(0) + RELAX
        wells = seg_parent.shape[1]
        wide[...] = jnp.zeros_like(wide)
        wide_parent[...] = jnp.zeros_like(wide_parent)
        wide_parent[:, :wells] = seg_parent[...]
        wide[0, :, :wells] = seg_cond[...]
        wide[1, :, :wells] = seg_target[...]
        right = lines(1) + RELAX * wide[1]
        parent = wide_parent[...]
        cond = wide[0]
        place = lax.broadcasted_iota(jnp.int32, (nseg, width), 0)
        inverse = [None] * nseg
        hits = [None] * nseg
        for s in range(nseg - 1, 0, -1):
            c = cond[s : s + 1]
            e = excess[s : s + 1]
            inverse[s] = 1.0 / (e + c)
            ratio = c * inverse[s]
            hits[s] = place == parent[s : s + 1]
            excess = excess + jnp.where(hits[s], ratio * e, 0.0)
            right = right + jnp.where(hits[s], ratio * right[s : s + 1], 0.0)
        answer = jnp.where(place == 0, right[0:1] / excess[0:1], 0.0)
        for s in range(1, nseg):
            above = jnp.sum(jnp.where(hits[s], answer, 0.0), axis=0, keepdims=True)
            value = (right[s : s + 1] + cond[s : s + 1] * above) * inverse[s]
            answer = jnp.where(place == s, value, answer)
        for j in range(layers):
            solved[j] = answer[j * slab : (j + 1) * slab]
        back[area] = solved[layer]
        for d in range(1, groups):
            to_source(d).start()

    above = jnp.minimum(level + 1, depth - 1)
    inner = jnp.where(level + 1 < depth, GEOMETRY[0], 0.0)
    carry = [jnp.zeros((1, ny), jnp.float32)] * 3
    column = lax.broadcasted_iota(jnp.int32, (chunk, ny), 1)
    for x in range(0, nx, chunk):
        span = slice(x, x + chunk)
        p = press[level, span, :]
        water = sats[0, level, span, :]
        gas_sat = sats[1, level, span, :]
        k = perm[level, span, :]
        lam = mobilities(water, gas_sat)
        here = (p, k, lam)
        y = min(x + chunk, nx - 1)
        row = slice(y, y + 1)
        next_k = perm[level, row, :] if x + chunk < nx else jnp.zeros((1, ny), jnp.float32)
        next_lam = mobilities(sats[0, level, row, :], sats[1, level, row, :])

        def shifted(value, end):
            return jnp.concatenate([value[1:], end], axis=0)

        there = (
            shifted(p, press[level, row, :]),
            shifted(k, next_k),
            tuple(shifted(lam[a], next_lam[a]) for a in range(3)),
        )
        flux = face_terms(GEOMETRY[1], here, there, None)
        total = []
        for a in range(3):
            total.append(flux[a] - jnp.concatenate([carry[a], flux[a][:-1]], axis=0))
        carry = [flux[a][chunk - 1 :] for a in range(3)]
        there = (
            pltpu.roll(p, ny - 1, 1),
            jnp.where(column < ny - 1, pltpu.roll(k, ny - 1, 1), 0.0),
            tuple(pltpu.roll(lam[a], ny - 1, 1) for a in range(3)),
        )
        flux = face_terms(GEOMETRY[2], here, there, None)
        for a in range(3):
            total[a] = total[a] + (flux[a] - pltpu.roll(flux[a], 1, 1))
        there = (
            press[above, span, :],
            perm[above, span, :],
            mobilities(sats[0, above, span, :], sats[1, above, span, :]),
        )
        flux = face_terms(inner, here, there, GRAVITY)
        volume = pore[0, span, :]
        old_water = old[0, 0, span, :]
        old_gas = old[1, 0, span, :]
        change = (
            water - old_water,
            (1.0 - water - gas_sat) - (1.0 - old_water - old_gas),
            gas_sat - old_gas,
        )
        for a in range(3):
            net = total[a] + (flux[a] - lower[a, span, :])
            lower[a, span, :] = flux[a]
            out[a, 0, span, :] = volume * change[a] + net

    @pl.when(level == depth - 1)
    def _():
        for side in range(2):
            rim(side).wait()

        def side_of(ref, side):
            return (
                ref[side, 0], ref[side, 3], mobilities(ref[side, 1], ref[side, 2])
            )

        low = face_terms(GEOMETRY[1], side_of(halos, 0), side_of(rims, 1), None)
        high = face_terms(GEOMETRY[1], side_of(rims, 0), side_of(halos, 1), None)
        for a in range(3):
            edges[a] = jnp.where(area > 0, low[a], 0.0)
            edges[3 + a] = jnp.where(area < groups - 1, high[a], 0.0)
        for d in range(1, groups):
            remote(
                back.at[area], back.at[lax.rem(area + groups - d, groups)],
                send_p.at[d], recv_p.at[d], areal_peer(d),
            ).wait_recv()
        table[...] = back[...]
        own_slab[...] = solved[layer]
        for d in range(1, groups):
            to_owner(d).wait_send()
            to_source(d).wait_send()
        for d in range(1, layers):
            to_layer(d).wait_send()

        @pl.when(layer < layers - 1)
        def _():
            for copy in planes(0):
                copy.wait_send()
            for copy in planes(1):
                copy.wait_recv()

        @pl.when(layer > 0)
        def _():
            for copy in planes(1):
                copy.wait_send()
            for copy in planes(0):
                copy.wait_recv()


def finish_kernel(
    slab, width, chunk, layers,
    flat_s, blocks_s, flat, seg, perf_press, perf_weight, table, own_slab, edges, below, over,
    base_hbm, sats_hbm, press, perm, out, well_out,
    source, source_b, adds, base_in, sats, sem,
):
    level = pl.program_id(0)
    depth = pl.num_programs(0)
    nx, ny = press.shape[1:]
    groups, slots = flat.shape
    layer = lax.axis_index("layer")

    def fetch(i):
        return (
            pltpu.make_async_copy(base_hbm.at[:, i], base_in.at[:, i], sem.at[0, i]),
            pltpu.make_async_copy(sats_hbm.at[:, i], sats.at[:, i], sem.at[1, i]),
        )

    @pl.when(level == 0)
    def _():
        for i in range(sem.shape[1]):
            for copy in fetch(i):
                copy.start()
        source[...] = jnp.zeros_like(source)
        source_b[...] = jnp.zeros_like(source_b)
        well_out[...] = own_slab[:, : well_out.shape[1]]
        target = panel_index(seg[...], slab, width)
        bins = lax.broadcasted_iota(jnp.int32, (slab * width, slots), 0)
        found = []
        for owner in range(groups):
            tab = table[owner]
            line = jnp.concatenate([tab[s : s + 1] for s in range(slab)], axis=1)
            left = jnp.concatenate(
                list(pieces(line)) + [jnp.zeros((5, slab * width), jnp.float32)], axis=0
            )
            hot = jnp.where(bins == target[owner : owner + 1], 1.0, 0.0).astype(jnp.bfloat16)
            value = jnp.dot(left.astype(jnp.bfloat16), hot, preferred_element_type=jnp.float32)
            found.append(value[0:1] + value[1:2] + value[2:3])
        rate = perf_weight[...] * (perf_press[...] - jnp.concatenate(found, axis=0))
        rate_t = jnp.transpose(tall(rate, LANES))
        lanes_t = jnp.transpose(tall(flat[...] % ny, LANES))
        lane = lax.broadcasted_iota(jnp.int32, (slots, ny), 1)
        for owner in range(groups):
            adds[owner * slots : (owner + 1) * slots, :] = jnp.where(
                lane == lanes_t[:, owner : owner + 1], rate_t[:, owner : owner + 1], 0.0
            )
        for owner in range(groups):
            for block in range(slots // BLOCK):
                base = owner * slots + block * BLOCK

                @pl.when(blocks_s[owner] > block)
                def _(base=base, owner=owner, block=block):
                    def step(i, carry):
                        for j in range(16):
                            at = i * 16 + j
                            number = split(flat_s[owner, block * BLOCK + at], ny)[0]
                            row = pl.ds(number, 1)
                            into = source if j % 2 == 0 else source_b
                            into[row, :] = into[row, :] + adds[pl.ds(base + at, 1), :]
                        return carry

                    lax.fori_loop(0, BLOCK // 16, step, 0)

    for copy in fetch(level):
        copy.wait()
    row_from = pl.multiple_of(level * nx, nx)
    for x in range(0, nx, chunk):
        span = slice(x, x + chunk)
        lam = mobilities(sats[0, level, span, :], sats[1, level, span, :])
        rows = pl.ds(row_from + x, chunk)
        well = source[rows, :] + source_b[rows, :]
        for a in range(3):
            out[a, 0, span, :] = base_in[a, level, span, :] + lam[a] * well
    for a in range(3):
        out[a, 0, 0:1, :] = out[a, 0, 0:1, :] - edges[a, pl.ds(level, 1), :]
        out[a, 0, nx - 1 : nx, :] = out[a, 0, nx - 1 : nx, :] + edges[3 + a, pl.ds(level, 1), :]

    def ends(halo, real, sign):
        for x in range(0, nx, chunk):
            span = slice(x, x + chunk)
            here = (press[0, span, :], perm[0, span, :], mobilities(sats[0, level, span, :], sats[1, level, span, :]))
            there = (halo[0, span, :], halo[3, span, :], mobilities(halo[1, span, :], halo[2, span, :]))
            pair = (here, there) if sign > 0 else (there, here)
            flux = face_terms(GEOMETRY[0], pair[0], pair[1], GRAVITY)
            for a in range(3):
                out[a, 0, span, :] = out[a, 0, span, :] + sign * jnp.where(real, flux[a], 0.0)

    @pl.when(level == 0)
    def _():
        ends(below, layer > 0, -1.0)

    @pl.when(level == depth - 1)
    def _():
        ends(over, layer < layers - 1, 1.0)


def on_device(
    pressure,
    saturations,
    old_saturations,
    permeability,
    pore_volume,
    perf_cell,
    perf_layer,
    perf_seg,
    perf_index,
    perf_blocks,
    seg_parent,
    seg_cond,
    seg_target,
):
    f32 = jnp.float32
    depth, nx, ny = pressure.shape
    groups, slots = perf_cell.shape[2:]
    layers = lax.axis_size("layer")
    wells, nseg = seg_parent.shape
    slab = nseg // layers
    width = -(-wells // LANES) * LANES
    halves = ny // LANES
    shape = jax.ShapeDtypeStruct
    vm = pl.BlockSpec(memory_space=VMEM)
    sm = pl.BlockSpec(memory_space=SMEM)

    flat = perf_layer[0, 0] * (nx * ny) + perf_cell[0, 0]
    seg = perf_seg[0, 0]
    count = perf_blocks[0, 0]
    tiles = 2 * slab * width // LANES
    sums, perf_press, perf_weight = pl.pallas_call(
        functools.partial(gather_kernel, slab, width, halves),
        out_shape=(
            shape((groups, tiles, LANES), f32),
            shape((groups, slots), f32),
            shape((groups, slots), f32),
        ),
        in_specs=[sm, sm] + [vm] * 5,
        out_specs=(vm, vm, vm),
        scratch_shapes=[VMEM((3, groups * slots, LANES), f32)],
        compiler_params=pltpu.CompilerParams(vmem_limit_bytes=VLIMIT),
        cost_estimate=pl.CostEstimate(flops=10**7, bytes_accessed=3 * 10**7, transcendentals=0),
        name="gather_perforations",
    )(
        flat, count, pressure.reshape(depth * nx, ny), saturations.reshape(2, depth * nx, ny),
        flat, seg, perf_index[0, 0],
    )

    dma = pltpu.SemaphoreType.DMA
    anywhere = pl.BlockSpec(memory_space=pl.ANY)
    plane = lambda n: pl.BlockSpec((n, 1, nx, ny), lambda i: (0, i, 0, 0))
    arbitrary = ("arbitrary",)
    base, below, over, table, own_slab, edges = pl.pallas_call(
        functools.partial(flow_kernel, groups, layers, slab, width, 16),
        grid=(depth,),
        out_shape=(
            shape((3, depth, nx, ny), f32),
            shape((4, nx, ny), f32),
            shape((4, nx, ny), f32),
            shape((groups, slab, width), f32),
            shape((slab, width), f32),
            shape((6, depth, ny), f32),
        ),
        in_specs=[vm] * 7 + [plane(2), pl.BlockSpec((1, nx, ny), lambda i: (i, 0, 0))],
        out_specs=(plane(3), anywhere, anywhere, vm, vm, vm),
        scratch_shapes=[
            VMEM((groups, tiles, LANES), f32),
            VMEM((layers, tiles, LANES), f32),
            VMEM((layers, slab, width), f32),
            VMEM((groups, slab, width), f32),
            VMEM((2, 4, depth, ny), f32),
            VMEM((2, 4, depth, ny), f32),
            VMEM((3, nx, ny), f32),
            VMEM((2, nseg, width), f32),
            VMEM((nseg, width), jnp.int32),
            dma((groups,)), dma((groups,)),
            dma((layers,)), dma((layers,)),
            dma((groups,)), dma((groups,)),
            dma((2,)), dma((2,)),
            dma((2, 4)), dma((2, 4)),
        ],
        compiler_params=pltpu.CompilerParams(
            collective_id=0, has_side_effects=True,
            vmem_limit_bytes=VLIMIT, dimension_semantics=arbitrary,
        ),
        cost_estimate=pl.CostEstimate(flops=10**8, bytes_accessed=6 * 10**7, transcendentals=0),
        name="block_flow",
    )(sums, seg_parent.T, seg_cond.T, seg_target.T, pressure, saturations, permeability, old_saturations, pore_volume)

    end_plane = pl.BlockSpec((1, nx, ny), lambda i: (jnp.where(i == depth - 1, i, 0), 0, 0))
    residual, well_pressure = pl.pallas_call(
        functools.partial(finish_kernel, slab, width, 16, layers),
        grid=(depth,),
        out_shape=(shape((3, depth, nx, ny), f32), shape((slab, wells), f32)),
        in_specs=[sm, sm] + [vm] * 9 + [anywhere, anywhere, end_plane, end_plane],
        out_specs=(plane(3), vm),
        scratch_shapes=[
            VMEM((depth * nx, ny), f32),
            VMEM((depth * nx, ny), f32),
            VMEM((groups * slots, ny), f32),
            VMEM((3, depth, nx, ny), f32),
            VMEM((2, depth, nx, ny), f32),
            dma((2, depth)),
        ],
        compiler_params=pltpu.CompilerParams(
            vmem_limit_bytes=VLIMIT, dimension_semantics=arbitrary
        ),
        cost_estimate=pl.CostEstimate(flops=10**7, bytes_accessed=2 * 10**7, transcendentals=0),
        name="wells_and_ends",
    )(
        flat, count, flat, seg, perf_press, perf_weight, table, own_slab, edges, below, over,
        base, saturations, pressure, permeability,
    )
    return residual, well_pressure.T


def solution(mesh):
    return jax.shard_map(
        on_device,
        mesh=mesh,
        in_specs=(
            P("layer", "areal", None),
            P(None, "layer", "areal", None),
            P(None, "layer", "areal", None),
            P("layer", "areal", None),
            P("layer", "areal", None),
            P("layer", "areal", None, None),
            P("layer", "areal", None, None),
            P("layer", "areal", None, None),
            P("layer", "areal", None, None),
            P("layer", "areal", None),
            P("areal", None),
            P("areal", None),
            P("areal", None),
        ),
        out_specs=(P(None, "layer", "areal", None), P("areal", "layer")),
        check_vma=False,
    )
```
